512 devices in a mesh: fsdp: 64 (over z, y_hi, core), replica: 8 (over y_lo, x).
Axes of the slice: x: 4, y: 8 (y_hi: 4, y_lo: 2; y = y_hi * 2 + y_lo), z: 8, core: 2. Of those that a mesh axis runs over, the one named last changes fastest.
Arguments:
- weights: bfloat16 [4096, 14336], P('fsdp'), may hold values from -5 to 5
- momentum: float32 [4096, 14336], P('fsdp', 'replica'), may hold values from -3 to 3
- hidden: bfloat16 [8, 7, 64, 14336], P('replica', None, 'fsdp'), may hold values from -8 to 8, as said below
- targets: bfloat16 [8, 7, 64, 4096], P('replica', None, None, 'fsdp'), may hold values from -24 to 24
Outputs:
- new_weights: bfloat16 [8, 4096, 14336], P('replica', 'fsdp')
- outer_weights: bfloat16 [4096, 14336], P('fsdp', 'replica')
- momentum_out: float32 [4096, 14336], P('fsdp', 'replica')
The draws below stay inside these ranges and needn't reach their ends.
Inputs may be any that keep to these rules, and one draw needn't show every extreme that they name: `hidden`: hidden activations of the layer.
All inputs are finite; a program needn't handle non-finite values.
Results may differ from the reference program's by a relative error of at most 0.013.
Values may be sent and summed in bfloat16 or wider, within the bound.
No kernel may reach another device: no remote copies, remote signals or barrier semaphores. Data moves between devices by JAX's collectives and lax.ppermute only.
A program may use at most 128 MiB of HBM per device.

```python
import math
import jax
import jax.numpy as jnp

D = 4096
FF = 14336
BEFORE = 3
STEPS = 7
TOKENS = 64
REPLICAS = 8


def draw_hidden(key, part):
    key = jax.random.fold_in(key, 11)
    first, second = jax.random.split(key)
    shape = (REPLICAS, STEPS, TOKENS, FF)
    base = jax.random.normal(first, shape, jnp.float32)
    spread = jnp.exp(jax.random.uniform(second, (FF,), jnp.float32, -0.7, 0.7))
    return jnp.clip(base * spread, -8.0, 8.0).astype(jnp.bfloat16)


def levels(key, dims, pieces, low, top_value):
    gain, own = 1.0, jax.random.fold_in(key, 6)
    for dim, shards_of in pieces:
        heights = jnp.exp(jax.random.uniform(jax.random.fold_in(own, dim), (shards_of,), jnp.float32, low / len(pieces), top_value / len(pieces)))
        gain = gain * jnp.repeat(heights, dims[dim] // shards_of).reshape([-1 if axis == dim else 1 for axis in range(len(dims))])
    return gain


def noise(stream_key, shape, scale, reach, cuts=(), kind=jnp.bfloat16):
    level = levels(stream_key, shape, cuts, -0.22, 0.18) if cuts else 1.0
    result = jax.random.normal(stream_key, shape, jnp.float32) * scale * level
    return jnp.minimum(jnp.maximum(result, -reach), reach).astype(kind)


def setup_inputs(seed: int = 0) -> dict:
    arg_keys = jax.random.split(jax.random.key(seed), 5)
    return {
        "weights": noise(arg_keys[0], (D, FF), 1.0, 5.0, ((0, 64),)),
        "momentum": noise(arg_keys[1], (D, FF), 0.5, 3.0, ((0, 64), (1, 8)), jnp.float32),
        "hidden": draw_hidden(jax.random.fold_in(arg_keys[4], 71), 0),
        "targets": noise(arg_keys[3], (REPLICAS, STEPS, TOKENS, D), 4.0, 24.0, ((0, 8), (3, 64))),
    }


inner_rate = 0.4
outer_rate = 0.7
momentum_rate = 0.9
mixing = 0.5

def inner_step(current, hidden_rows, target_rows):
    inverse_root = 1.0 / math.sqrt(FF)
    projected = jnp.dot(hidden_rows, current.T, preferred_element_type=jnp.float32) * inverse_root
    residual = (projected - target_rows.astype(jnp.float32)).astype(jnp.bfloat16)
    update = jnp.dot(residual.T, hidden_rows, preferred_element_type=jnp.float32)
    return (current.astype(jnp.float32) - inner_rate * inverse_root * update).astype(jnp.bfloat16)

def reference(weights, momentum, hidden, targets):
    early_list = []
    code_total = jnp.zeros((D, FF), jnp.float32)
    for group in range(REPLICAS):
        current = weights
        for number in range(BEFORE):
            current = inner_step(current, hidden[group, number], targets[group, number])
        early_list.append(current)
        pseudo = weights.astype(jnp.float32) - current.astype(jnp.float32)
        encoded = pseudo.astype(jnp.bfloat16)
        code_total = code_total + encoded.astype(jnp.float32)
    average = code_total / REPLICAS
    momentum_out = momentum_rate * momentum + average
    outer_weights = (weights.astype(jnp.float32) - outer_rate * (average + momentum_rate * momentum_out)).astype(jnp.bfloat16)
    results = []
    for group in range(REPLICAS):
        current = early_list[group]
        for number in range(BEFORE, STEPS):
            current = inner_step(current, hidden[group, number], targets[group, number])
        mixed = mixing * current.astype(jnp.float32) + (1.0 - mixing) * outer_weights.astype(jnp.float32)
        results.append(mixed.astype(jnp.bfloat16))
    new_weights = jnp.stack(results, axis=0)
    return (new_weights, outer_weights, momentum_out)
```

```python
import functools
import math

import jax
import jax.numpy as jnp
from jax import lax
from jax.experimental import pallas as pl
from jax.experimental.pallas import tpu as pltpu
from jax.sharding import Mesh
from jax.sharding import PartitionSpec as P

BEFORE = 3
DURING = 4

inner_rate = 0.4
outer_rate = 0.7
momentum_rate = 0.9
mixing = 0.5

PIECES = 8
MESH_AXES = ("z", "y", "core", "y_lo", "x")
FSDP = ("z", "y", "core")
REPLICA = ("y_lo", "x")
VMEM_LIMIT = 48 * 1024 * 1024


def window_kernel(steps, early, *refs):
    if early:
        hidden, weights, targets, out, hs, ws, outs, hidden_sem, weights_sem, out_sem = refs
    else:
        (hidden, weights, encoded, targets, out, hs, ws, es, outs, hidden_sem, weights_sem,
         encoded_sem, out_sem) = refs
    rows = hidden.shape[0]
    width = hs.shape[2]
    features = ws.shape[1]
    inverse_root = 1.0 / math.sqrt(width * PIECES)

    def columns(piece):
        return pl.ds(piece * width, width)

    def hidden_copy(piece):
        return pltpu.make_async_copy(
            hidden.at[:, columns(piece)], hs.at[piece], hidden_sem.at[piece])

    def weights_copy(piece):
        return pltpu.make_async_copy(
            weights.at[:, columns(piece)], ws.at[piece], weights_sem.at[piece])

    def encoded_copy(piece):
        return pltpu.make_async_copy(encoded.at[piece], es.at[piece], encoded_sem.at[piece])

    def out_copy(piece):
        target = out.at[piece] if early else out.at[:, columns(piece)]
        return pltpu.make_async_copy(outs.at[piece], target, out_sem.at[piece])

    for piece in range(PIECES):
        hidden_copy(piece).start()
        weights_copy(piece).start()
        if not early:
            encoded_copy(piece).start()

    across = (((1,), (1,)), ((), ()))

    def gather_products(piece, carry):
        projected, gram = carry
        weights_copy(piece).wait()
        current = ws[piece]
        if not early:
            encoded_copy(piece).wait()
            current = (current.astype(jnp.float32) - es[piece].astype(jnp.float32)).astype(
                jnp.bfloat16)
            ws[piece] = current
        hidden_copy(piece).wait()
        block = hs[piece]
        projected += lax.dot_general(block, current, across, preferred_element_type=jnp.float32)
        gram += lax.dot_general(block, block, across, preferred_element_type=jnp.float32)
        return projected, gram

    projected, gram = lax.fori_loop(
        0, PIECES, gather_products,
        (jnp.zeros((rows, features), jnp.float32), jnp.zeros((rows, rows), jnp.float32)))

    gram_high = gram.astype(jnp.bfloat16)
    gram_low = (gram - gram_high.astype(jnp.float32)).astype(jnp.bfloat16)
    step_of = lax.broadcasted_iota(jnp.int32, (rows, features), 0) % steps
    wanted = targets[...].astype(jnp.float32)
    scaled = projected * inverse_root
    residual = jnp.zeros((rows, features), jnp.float32)
    for number in range(steps):
        moved = scaled
        if number:
            short = residual.astype(jnp.bfloat16)
            product = jnp.dot(gram_high, short, preferred_element_type=jnp.float32)
            product += jnp.dot(gram_low, short, preferred_element_type=jnp.float32)
            moved = scaled - (inner_rate * inverse_root * inverse_root) * product
        fresh = (moved - wanted).astype(jnp.bfloat16).astype(jnp.float32)
        residual = jnp.where(step_of == number, fresh, residual)
    turned = residual.T.astype(jnp.bfloat16)

    def write(piece, carry):
        update = (inner_rate * inverse_root) * jnp.dot(
            turned, hs[piece], preferred_element_type=jnp.float32)
        if early:
            outs[piece] = update.astype(jnp.bfloat16)
        else:
            outs[piece] = (ws[piece].astype(jnp.float32) - update).astype(jnp.bfloat16)
        out_copy(piece).start()
        return carry

    lax.fori_loop(0, PIECES, write, 0)
    for piece in range(PIECES):
        out_copy(piece).wait()


def run_window(steps, hidden, weights, targets, encoded=None):
    early = encoded is None
    rows = hidden.shape[0]
    features, columns = weights.shape
    width = columns // PIECES
    anywhere = pl.BlockSpec(memory_space=pl.ANY)
    whole = pl.BlockSpec(memory_space=pltpu.VMEM)
    held = pltpu.VMEM((PIECES, features, width), jnp.bfloat16)
    semaphores = pltpu.SemaphoreType.DMA((PIECES,))
    count = 1 if early else 2
    operands = (hidden, weights, targets) if early else (hidden, weights, encoded, targets)
    return pl.pallas_call(
        functools.partial(window_kernel, steps, early),
        out_shape=jax.ShapeDtypeStruct(
            (PIECES, features, width) if early else (features, columns), jnp.bfloat16),
        in_specs=[anywhere] * (1 + count) + [whole],
        out_specs=anywhere,
        scratch_shapes=[pltpu.VMEM((PIECES, rows, width), jnp.bfloat16)]
        + [held] * (1 + count) + [semaphores] * (2 + count),
        compiler_params=pltpu.CompilerParams(vmem_limit_bytes=VMEM_LIMIT),
        cost_estimate=pl.CostEstimate(
            flops=2 * rows * columns * (rows + 2 * features),
            bytes_accessed=2 * columns * (rows + (2 + count) * features), transcendentals=0),
        name="early_window" if early else "late_window",
    )(*operands)


def mix_kernel(late, outer, out):
    out[...] = (
        mixing * late[...].astype(jnp.float32) + (1.0 - mixing) * outer[...].astype(jnp.float32)
    ).astype(jnp.bfloat16)


def mix(late, outer):
    features, columns = late.shape
    width = columns // PIECES
    flat = pl.BlockSpec((features, width), lambda piece: (0, piece))
    return pl.pallas_call(
        mix_kernel,
        grid=(PIECES,),
        out_shape=jax.ShapeDtypeStruct((features, columns), jnp.bfloat16),
        in_specs=[flat, pl.BlockSpec((None, features, width), lambda piece: (piece, 0, 0))],
        out_specs=flat,
        cost_estimate=pl.CostEstimate(
            flops=3 * features * columns, bytes_accessed=6 * features * columns,
            transcendentals=0),
        name="mix",
    )(late, outer)


def body(weights, momentum, hidden, targets):
    features, columns = weights.shape
    width = columns // PIECES
    groups = lax.axis_size(REPLICA)
    lanes = lax.axis_size("y")
    outer_ring = lax.axis_size(("z", "core"))
    own = hidden.reshape(BEFORE + DURING, PIECES, width)

    def gathered(part, steps):
        near = lax.all_gather(part.reshape(steps * PIECES, width), "y", axis=0, tiled=True)
        if steps * lanes % 8 == 0:
            near = near.reshape(lanes * steps, columns)
        far = lax.all_gather(near, ("z", "core"), axis=0, tiled=True)
        return far.reshape(outer_ring * lanes * steps, columns)

    def target_rows(part, steps):
        parts = part.reshape(steps, lax.axis_size("z"), lanes, lax.axis_size("core"), features)
        return parts.transpose(1, 3, 2, 0, 4).reshape(-1, features)

    early_hidden = gathered(own[:BEFORE], BEFORE)
    late_hidden = gathered(own[BEFORE:], DURING)
    early_targets = target_rows(targets[0, :BEFORE], BEFORE)
    late_targets = target_rows(targets[0, BEFORE:], DURING)

    encoded = run_window(BEFORE, early_hidden, weights, early_targets)
    received = lax.all_to_all(encoded, REPLICA, split_axis=0, concat_axis=0, tiled=True)
    average = jnp.sum(received.astype(jnp.float32), axis=0) / groups
    momentum_out = momentum_rate * momentum + average
    start_rows = lax.dynamic_slice_in_dim(
        weights, lax.axis_index(REPLICA) * width, width, 1
    ).astype(jnp.float32)
    outer_shard = (start_rows - outer_rate * (average + momentum_rate * momentum_out)).astype(
        jnp.bfloat16
    )
    outer_full = lax.all_to_all(
        jnp.broadcast_to(outer_shard, (groups, features, width)),
        REPLICA, split_axis=0, concat_axis=0, tiled=True)

    late = run_window(DURING, late_hidden, weights, late_targets, encoded)
    new_weights = mix(late, outer_full)[None]
    return (new_weights, outer_shard, momentum_out)


def solution(mesh):
    fine = Mesh(mesh.devices.reshape(8, 4, 2, 2, 4), MESH_AXES)
    placed = (
        P(FSDP, None),
        P(FSDP, REPLICA),
        P(REPLICA, None, FSDP, None),
        P(REPLICA, None, None, FSDP),
    )
    return jax.shard_map(
        body,
        mesh=fine,
        in_specs=placed,
        out_specs=(P(REPLICA, FSDP, None), P(FSDP, REPLICA), P(FSDP, REPLICA)),
        check_vma=False,
    )
```

```python
import functools
import math

import jax
import jax.numpy as jnp
from jax import lax
from jax.experimental import pallas as pl
from jax.experimental.pallas import tpu as pltpu
from jax.sharding import Mesh
from jax.sharding import PartitionSpec as P

BEFORE = 3
DURING = 4

inner_rate = 0.4
outer_rate = 0.7
momentum_rate = 0.9
mixing = 0.5

MESH_AXES = ("z", "y", "core", "y_lo", "x")
FSDP = ("z", "y", "core")
REPLICA = ("y_lo", "x")
RING = ("z", "core")
PIECES = 8
VMEM_LIMIT = 48 * 1024 * 1024
ACROSS = (((1,), (1,)), ((), ()))

def split_dot(high, low, short):
    product = jnp.dot(high, short, preferred_element_type=jnp.float32)
    return product + jnp.dot(low, short, preferred_element_type=jnp.float32)

def early_kernel(steps, hidden, weights, targets, out, hs, ws, outs, gram_ref, proj_ref, hidden_sem, weights_sem, out_sem):
    rows = hidden.shape[0]
    width = hs.shape[2]
    count = hs.shape[0]
    features = weights.shape[0]
    inverse_root = 1.0 / math.sqrt(weights.shape[1])
    def hidden_copy(piece):
        return pltpu.make_async_copy(hidden.at[:, pl.ds(piece * width, width)], hs.at[piece], hidden_sem.at[piece])
    def weights_copy(piece, side):
        return pltpu.make_async_copy(weights.at[:, pl.ds((side * count + piece) * width, width)],
            ws.at[piece, pl.ds(side * features, features)], weights_sem.at[side, piece])
    def out_copy(piece):
        return pltpu.make_async_copy(outs.at[piece], out.at[piece], out_sem.at[piece])
    for piece in range(count):
        hidden_copy(piece).start()
        weights_copy(piece, 0).start()
        weights_copy(piece, 1).start()
    proj_ref[...] = jnp.zeros_like(proj_ref)
    gram_ref[...] = jnp.zeros_like(gram_ref)
    def products(piece, carry):
        weights_copy(piece, 0).wait()
        weights_copy(piece, 1).wait()
        hidden_copy(piece).wait()
        block = hs[piece]
        proj_ref[...] += lax.dot_general(block, ws[piece], ACROSS, preferred_element_type=jnp.float32)
        gram_ref[...] += lax.dot_general(block, block, ACROSS, preferred_element_type=jnp.float32)
        return carry
    lax.fori_loop(0, count, products, 0)
    row = lax.broadcasted_iota(jnp.int32, (rows, features), 0)
    left = row % 2 == 0
    step_of = (row // 2) % steps
    def both(x):
        return x + jnp.where(left, pltpu.roll(x, rows - 1, 0), pltpu.roll(x, 1, 0))
    scaled = both(jnp.where(left, proj_ref[:, :features], proj_ref[:, features:])) * inverse_root
    gram = gram_ref[...]
    same = (lax.broadcasted_iota(jnp.int32, (rows, rows), 0) + lax.broadcasted_iota(jnp.int32, (rows, rows), 1)) % 2 == 0
    gram = jnp.where(same, gram, 0.0)
    high = gram.astype(jnp.bfloat16)
    low = (gram - high.astype(jnp.float32)).astype(jnp.bfloat16)
    wanted = targets[...].astype(jnp.float32)
    residual = jnp.zeros((rows, features), jnp.float32)
    for number in range(steps):
        moved = scaled
        if number:
            moved = scaled - (inner_rate * inverse_root * inverse_root) * both(split_dot(high, low, residual.astype(jnp.bfloat16)))
        fresh = (moved - wanted).astype(jnp.bfloat16).astype(jnp.float32)
        residual = jnp.where(step_of == number, fresh, residual)
    turned = jnp.concatenate([jnp.where(left, residual, 0.0), jnp.where(left, 0.0, residual)], axis=1).T.astype(jnp.bfloat16)
    def write(piece, carry):
        update = (inner_rate * inverse_root) * jnp.dot(turned, hs[piece], preferred_element_type=jnp.float32)
        encoded = update.astype(jnp.bfloat16)
        outs[piece] = encoded[:features]
        outs[count + piece] = encoded[features:]
        out_copy(piece).start()
        out_copy(count + piece).start()
        return carry
    lax.fori_loop(0, count, write, 0)
    for piece in range(PIECES):
        out_copy(piece).wait()

def early_window(steps, hidden, weights, targets):
    rows = hidden.shape[0]
    features, columns = weights.shape
    width = columns // PIECES
    count = PIECES // 2
    anywhere = pl.BlockSpec(memory_space=pltpu.HBM)
    return pl.pallas_call(
        functools.partial(early_kernel, steps),
        out_shape=pltpu.HBM((PIECES, features, width), jnp.bfloat16),
        in_specs=[anywhere, anywhere, pl.BlockSpec(memory_space=pltpu.VMEM)],
        out_specs=anywhere,
        scratch_shapes=[
            pltpu.VMEM((count, rows, width), jnp.bfloat16),
            pltpu.VMEM((count, 2 * features, width), jnp.bfloat16),
            pltpu.VMEM((PIECES, features, width), jnp.bfloat16),
            pltpu.VMEM((rows, rows), jnp.float32),
            pltpu.VMEM((rows, 2 * features), jnp.float32),
            pltpu.SemaphoreType.DMA((count,)),
            pltpu.SemaphoreType.DMA((2, count)),
            pltpu.SemaphoreType.DMA((PIECES,)),
        ],
        compiler_params=pltpu.CompilerParams(vmem_limit_bytes=VMEM_LIMIT),
        cost_estimate=pl.CostEstimate(flops=2*rows*columns*rows, bytes_accessed=rows*columns+4*features*columns, transcendentals=0),
        name="early_window")(hidden, weights, targets)

def late_kernel(steps, hidden, weights, encoded, targets, out, hs, ws, es, outs, gram_ref, proj_ref, hidden_sem, weights_sem, enc_sem, out_sem):
    rows = hidden.shape[0]
    width = hs.shape[2]
    features = weights.shape[0]
    inverse_root = 1.0 / math.sqrt(weights.shape[1])
    def hidden_copy(piece):
        return pltpu.make_async_copy(hidden.at[:, pl.ds(piece * width, width)], hs.at[piece], hidden_sem.at[piece])
    def weights_copy(piece):
        return pltpu.make_async_copy(weights.at[:, pl.ds(piece * width, width)], ws.at[piece], weights_sem.at[piece])
    def enc_copy(piece):
        return pltpu.make_async_copy(encoded.at[piece], es.at[piece], enc_sem.at[piece])
    def out_copy(piece):
        return pltpu.make_async_copy(outs.at[piece], out.at[:, pl.ds(piece * width, width)], out_sem.at[piece])
    for piece in range(PIECES):
        weights_copy(piece).start()
        enc_copy(piece).start()
        hidden_copy(piece).start()
    proj_ref[...] = jnp.zeros_like(proj_ref)
    gram_ref[...] = jnp.zeros_like(gram_ref)
    def products(piece, carry):
        weights_copy(piece).wait()
        enc_copy(piece).wait()
        current = (ws[piece].astype(jnp.float32) - es[piece].astype(jnp.float32)).astype(jnp.bfloat16)
        ws[piece] = current
        hidden_copy(piece).wait()
        block = hs[piece]
        proj_ref[...] += lax.dot_general(block, current, ACROSS, preferred_element_type=jnp.float32)
        gram_ref[...] += lax.dot_general(block, block, ACROSS, preferred_element_type=jnp.float32)
        return carry
    lax.fori_loop(0, PIECES, products, 0)
    step_of = lax.broadcasted_iota(jnp.int32, (rows, features), 0) % steps
    scaled = proj_ref[...] * inverse_root
    gram = gram_ref[...]
    high = gram.astype(jnp.bfloat16)
    low = (gram - high.astype(jnp.float32)).astype(jnp.bfloat16)
    wanted = targets[...].astype(jnp.float32)
    residual = jnp.zeros((rows, features), jnp.float32)
    for number in range(steps):
        moved = scaled
        if number:
            moved = scaled - (inner_rate * inverse_root * inverse_root) * split_dot(high, low, residual.astype(jnp.bfloat16))
        fresh = (moved - wanted).astype(jnp.bfloat16).astype(jnp.float32)
        residual = jnp.where(step_of == number, fresh, residual)
    turned = residual.T.astype(jnp.bfloat16)
    def write(piece, carry):
        update = (inner_rate * inverse_root) * jnp.dot(turned, hs[piece], preferred_element_type=jnp.float32)
        outs[piece] = (ws[piece].astype(jnp.float32) - update).astype(jnp.bfloat16)
        out_copy(piece).start()
        return carry
    lax.fori_loop(0, PIECES, write, 0)
    for piece in range(PIECES):
        out_copy(piece).wait()

def late_window(steps, hidden, weights, encoded, targets):
    rows = hidden.shape[0]
    features, columns = weights.shape
    width = columns // PIECES
    anywhere = pl.BlockSpec(memory_space=pltpu.HBM)
    held = pltpu.VMEM((PIECES, features, width), jnp.bfloat16)
    sems = pltpu.SemaphoreType.DMA((PIECES,))
    return pl.pallas_call(
        functools.partial(late_kernel, steps),
        out_shape=pltpu.HBM((features, columns), jnp.bfloat16),
        in_specs=[anywhere]*3+[pl.BlockSpec(memory_space=pltpu.VMEM)],
        out_specs=anywhere,
        scratch_shapes=[pltpu.VMEM((PIECES, rows, width), jnp.bfloat16), held, held, held,
            pltpu.VMEM((rows, rows), jnp.float32), pltpu.VMEM((rows, features), jnp.float32),
            sems, sems, sems, sems],
        compiler_params=pltpu.CompilerParams(vmem_limit_bytes=VMEM_LIMIT),
        cost_estimate=pl.CostEstimate(flops=2*rows*columns*(rows+2*features), bytes_accessed=2*columns*(rows+4*features), transcendentals=0),
        name="late_window")(hidden, weights, encoded, targets)

def outer_kernel(offset, received, momentum, weights, shard, momentum_out, copies, rs, ms, ws, os_, in_sem, out_sem):
    groups = received.shape[0]
    half = received.shape[1]
    width = received.shape[2]
    begin = pl.multiple_of(offset[0] * width, 128)
    loads = [pltpu.make_async_copy(momentum, ms, in_sem.at[groups]),
             pltpu.make_async_copy(weights.at[:, pl.ds(begin, width)], ws, in_sem.at[groups + 1])]
    loads += [pltpu.make_async_copy(received.at[g], rs.at[g], in_sem.at[g]) for g in range(groups)]
    for load in loads: load.start()
    total = jnp.zeros((half, width), jnp.float32)
    for load in loads: load.wait()
    for g in range(groups):
        total += rs[g].astype(jnp.float32)
    average = total / groups
    fresh = momentum_rate * ms[...] + average
    ms[...] = fresh
    os_[...] = (ws[...].astype(jnp.float32) - outer_rate * (average + momentum_rate * fresh)).astype(jnp.bfloat16)
    stores = [pltpu.make_async_copy(os_, copies.at[g], out_sem.at[g]) for g in range(groups)]
    stores += [pltpu.make_async_copy(os_, shard, out_sem.at[groups]),
               pltpu.make_async_copy(ms, momentum_out, out_sem.at[groups + 1])]
    for store in stores: store.start()
    for store in stores: store.wait()

def outer_step(offset, received, momentum, weights):
    groups, half, width = received.shape
    anywhere = pl.BlockSpec(memory_space=pltpu.HBM)
    sems = pltpu.SemaphoreType.DMA((groups + 2,))
    return pl.pallas_call(
        outer_kernel,
        out_shape=(pltpu.HBM(momentum.shape, jnp.bfloat16), pltpu.HBM(momentum.shape, jnp.float32),
                   pltpu.HBM(received.shape, jnp.bfloat16)),
        in_specs=[pl.BlockSpec(memory_space=pltpu.SMEM)] + [anywhere]*3,
        out_specs=(anywhere,)*3,
        scratch_shapes=[pltpu.VMEM(received.shape, jnp.bfloat16), pltpu.VMEM((half, width), jnp.float32),
            pltpu.VMEM((half, width), jnp.bfloat16), pltpu.VMEM((half, width), jnp.bfloat16), sems, sems],
        compiler_params=pltpu.CompilerParams(vmem_limit_bytes=VMEM_LIMIT),
        cost_estimate=pl.CostEstimate(flops=groups*half*width, bytes_accessed=4*groups*half*width, transcendentals=0),
        name="outer_step")(offset, received, momentum, weights)

def mix_kernel(late, outer, out, ls, os_, ns, late_sem, outer_sem, out_sem):
    width = ls.shape[2]
    def late_copy(p): return pltpu.make_async_copy(late.at[:, pl.ds(p * width, width)], ls.at[p], late_sem.at[p])
    def outer_copy(p): return pltpu.make_async_copy(outer.at[p], os_.at[p], outer_sem.at[p])
    def out_copy(p): return pltpu.make_async_copy(ns.at[p], out.at[:, pl.ds(p * width, width)], out_sem.at[p])
    for p in range(PIECES):
        late_copy(p).start(); outer_copy(p).start()
    for p in range(PIECES):
        late_copy(p).wait(); outer_copy(p).wait()
        ns[p] = (mixing * ls[p].astype(jnp.float32) + (1.0 - mixing) * os_[p].astype(jnp.float32)).astype(jnp.bfloat16)
        out_copy(p).start()
    for p in range(PIECES):
        out_copy(p).wait()

def mix(late, outer):
    features, columns = late.shape
    width = columns // PIECES
    anywhere = pl.BlockSpec(memory_space=pltpu.HBM)
    held = pltpu.VMEM((PIECES, features, width), jnp.bfloat16)
    sems = pltpu.SemaphoreType.DMA((PIECES,))
    return pl.pallas_call(mix_kernel, out_shape=pltpu.HBM((features, columns), jnp.bfloat16),
        in_specs=[anywhere]*2, out_specs=anywhere,
        scratch_shapes=[held]*3+[sems]*3,
        compiler_params=pltpu.CompilerParams(vmem_limit_bytes=VMEM_LIMIT),
        cost_estimate=pl.CostEstimate(flops=3*features*columns, bytes_accessed=6*features*columns, transcendentals=0),
        name="mix")(late, outer)


def body(weights, momentum, hidden, targets):
    features, columns = weights.shape
    width = columns // PIECES
    lanes = lax.axis_size("y")
    depth = lax.axis_size("z")
    cores = lax.axis_size("core")
    own = hidden.reshape(BEFORE + DURING, PIECES, width)

    def near_rows(part, steps):
        return lax.all_gather(part.reshape(steps * PIECES, width), "y", axis=0, tiled=True)

    def target_rows(part, steps):
        parts = part.reshape(steps, depth, lanes, cores, features)
        return parts.transpose(1, 3, 2, 0, 4).reshape(-1, features)

    early_near = near_rows(own[:BEFORE], BEFORE).reshape(2 * lanes * BEFORE, columns // 2)
    early_hidden = lax.all_gather(early_near, RING, axis=0, tiled=True)
    late_near = near_rows(own[BEFORE:], DURING).reshape(lanes * DURING, columns)
    late_hidden = lax.all_gather(late_near, RING, axis=0, tiled=True)
    early_targets = jnp.repeat(target_rows(targets[0, :BEFORE], BEFORE), 2, axis=0)
    late_targets = target_rows(targets[0, BEFORE:], DURING)

    encoded = early_window(BEFORE, early_hidden, weights, early_targets)

    def swap(x):
        moved = lax.all_to_all(x, REPLICA, split_axis=0, concat_axis=0, tiled=True)
        return pltpu.with_memory_space_constraint(moved, pltpu.HBM)

    place = lax.axis_index(REPLICA).astype(jnp.int32)[None]
    outer_shard, momentum_out, copies = outer_step(place, swap(encoded), momentum, weights)
    outer = swap(copies)

    late = late_window(DURING, late_hidden, weights, encoded, late_targets)
    new_weights = mix(late, outer)[None]
    return (new_weights, outer_shard, momentum_out)


def solution(mesh):
    fine = Mesh(mesh.devices.reshape(8, 4, 2, 2, 4), MESH_AXES)
    placed = (
        P(FSDP, None),
        P(FSDP, REPLICA),
        P(REPLICA, None, FSDP, None),
        P(REPLICA, None, None, FSDP),
    )
    return jax.shard_map(
        body,
        mesh=fine,
        in_specs=placed,
        out_specs=(P(REPLICA, FSDP, None), P(FSDP, REPLICA), P(FSDP, REPLICA)),
        check_vma=False,
    )
```

```python
import functools
import math

import jax
import jax.numpy as jnp
from jax import lax
from jax.experimental import pallas as pl
from jax.experimental.pallas import tpu as pltpu
from jax.sharding import Mesh
from jax.sharding import PartitionSpec as P

BEFORE = 3
DURING = 4

inner_rate = 0.4
outer_rate = 0.7
momentum_rate = 0.9
mixing = 0.5

MESH_AXES = ("z", "y", "core", "y_lo", "x")
FSDP = ("z", "y", "core")
REPLICA = ("y_lo", "x")
RING = ("z", "core")
PIECES = 8
VMEM_LIMIT = 48 * 1024 * 1024
AHEAD = 3
ACROSS = (((1,), (1,)), ((), ()))


def in_order(count, start, use, unroll):
    for piece in range(min(AHEAD, count)):
        start(piece)

    def turn(piece, carry):
        @pl.when(piece + AHEAD < count)
        def _():
            start(piece + AHEAD)

        use(piece)
        return carry

    lax.fori_loop(0, count, turn, 0, unroll=unroll)


def solve(steps, step_of, scaled, gram, wanted, moved_by, total):
    high = gram.astype(jnp.bfloat16)
    low = (gram - high.astype(jnp.float32)).astype(jnp.bfloat16)
    residual = jnp.zeros_like(scaled)
    for number in range(steps):
        moved = scaled
        if number:
            short = residual.astype(jnp.bfloat16)
            product = jnp.dot(short, high, preferred_element_type=jnp.float32)
            product += jnp.dot(short, low, preferred_element_type=jnp.float32)
            moved = scaled - moved_by * total(product)
        fresh = (moved - wanted).astype(jnp.bfloat16).astype(jnp.float32)
        residual = jnp.where(step_of == number, fresh, residual)
    return residual


def early_kernel(steps, hidden, weights, targets, out, held, outs, both_ref, hidden_sem,
                 weights_sem, out_sem):
    rows = hidden.shape[0]
    count, _, width = held.shape
    features = weights.shape[0]
    top = 2 * features
    inverse_root = 1.0 / math.sqrt(weights.shape[1])

    def copies(piece):
        yield pltpu.make_async_copy(
            hidden.at[:, pl.ds(piece * width, width)], held.at[piece, pl.ds(top, rows)],
            hidden_sem.at[piece])
        for side in range(2):
            yield pltpu.make_async_copy(
                weights.at[:, pl.ds((side * count + piece) * width, width)],
                held.at[piece, pl.ds(side * features, features)], weights_sem.at[side, piece])

    def out_copy(piece):
        return pltpu.make_async_copy(outs.at[piece], out.at[piece], out_sem.at[piece])

    def start(piece):
        for copy in copies(piece):
            copy.start()

    def products(piece):
        for copy in copies(piece):
            copy.wait()
        both_ref[...] += lax.dot_general(
            held[piece, top:], held[piece], ACROSS, preferred_element_type=jnp.float32)

    both_ref[...] = jnp.zeros_like(both_ref)
    in_order(count, start, products, count)

    column = lax.broadcasted_iota(jnp.int32, (features, rows), 1)
    left = column % 2 == 0

    def total(x):
        return x + jnp.where(left, pltpu.roll(x, rows - 1, 1), pltpu.roll(x, 1, 1))

    projected = both_ref[:, :top].T
    scaled = total(jnp.where(left, projected[:features], projected[features:])) * inverse_root
    apart = (lax.broadcasted_iota(jnp.int32, (rows, rows), 0)
             + lax.broadcasted_iota(jnp.int32, (rows, rows), 1)) % 2
    gram = jnp.where(apart == 0, both_ref[:, top:], 0.0)
    residual = solve(steps, (column // 2) % steps, scaled, gram, targets[...].astype(jnp.float32),
                     inner_rate * inverse_root * inverse_root, total)
    factors = jnp.concatenate(
        [jnp.where(left, residual, 0.0), jnp.where(left, 0.0, residual)], axis=0
    ).astype(jnp.bfloat16)

    def write(piece, carry):
        update = (inner_rate * inverse_root) * jnp.dot(
            factors, held[piece, top:], preferred_element_type=jnp.float32)
        encoded = update.astype(jnp.bfloat16)
        outs[piece] = encoded[:features]
        outs[count + piece] = encoded[features:]
        out_copy(piece).start()
        out_copy(count + piece).start()
        return carry

    lax.fori_loop(0, count, write, 0, unroll=4)
    for piece in range(PIECES):
        out_copy(piece).wait()


def early_window(steps, hidden, weights, targets):
    rows = hidden.shape[0]
    features, columns = weights.shape
    width = columns // PIECES
    count = PIECES // 2
    anywhere = pl.BlockSpec(memory_space=pl.ANY)
    return pl.pallas_call(
        functools.partial(early_kernel, steps),
        out_shape=pltpu.HBM((PIECES, features, width), jnp.bfloat16),
        in_specs=[anywhere, anywhere, pl.BlockSpec(memory_space=pltpu.VMEM)],
        out_specs=anywhere,
        scratch_shapes=[
            pltpu.VMEM((count, 2 * features + rows, width), jnp.bfloat16),
            pltpu.VMEM((PIECES, features, width), jnp.bfloat16),
            pltpu.VMEM((rows, 2 * features + rows), jnp.float32),
            pltpu.SemaphoreType.DMA((count,)),
            pltpu.SemaphoreType.DMA((2, count)),
            pltpu.SemaphoreType.DMA((PIECES,)),
        ],
        compiler_params=pltpu.CompilerParams(vmem_limit_bytes=VMEM_LIMIT),
        cost_estimate=pl.CostEstimate(
            flops=rows * columns * (rows + 4 * features),
            bytes_accessed=columns * (rows + 4 * features), transcendentals=0),
        name="early_window",
    )(hidden, weights, targets)


def late_kernel(steps, hidden, base, targets, out, held, outs, both_ref, hidden_sem, base_sem,
                out_sem):
    rows = hidden.shape[0]
    count, features, width = base.shape
    inverse_root = 1.0 / math.sqrt(hidden.shape[1])

    def copies(piece):
        yield pltpu.make_async_copy(
            hidden.at[:, pl.ds(piece * width, width)], held.at[piece, pl.ds(features, rows)],
            hidden_sem.at[piece])
        yield pltpu.make_async_copy(
            base.at[piece], held.at[piece, pl.ds(0, features)], base_sem.at[piece])

    def out_copy(piece):
        return pltpu.make_async_copy(
            outs.at[piece], out.at[:, pl.ds(piece * width, width)], out_sem.at[piece])

    def start(piece):
        for copy in copies(piece):
            copy.start()

    def products(piece):
        for copy in copies(piece):
            copy.wait()
        both_ref[...] += lax.dot_general(
            held[piece], held[piece, features:], ACROSS, preferred_element_type=jnp.float32)

    both_ref[...] = jnp.zeros_like(both_ref)
    in_order(count, start, products, 1)

    step_of = lax.broadcasted_iota(jnp.int32, (features, rows), 1) % steps
    residual = solve(steps, step_of, both_ref[:features] * inverse_root, both_ref[features:],
                     targets[...].astype(jnp.float32), inner_rate * inverse_root * inverse_root,
                     lambda x: x)
    factors = residual.astype(jnp.bfloat16)

    def write(piece, carry):
        update = (inner_rate * inverse_root) * jnp.dot(
            factors, held[piece, features:], preferred_element_type=jnp.float32)
        outs[piece] = (held[piece, :features].astype(jnp.float32) - update).astype(jnp.bfloat16)
        out_copy(piece).start()
        return carry

    lax.fori_loop(0, count, write, 0, unroll=4)
    for piece in range(count):
        out_copy(piece).wait()


def late_window(steps, hidden, base, targets):
    rows, columns = hidden.shape
    count, features, width = base.shape
    anywhere = pl.BlockSpec(memory_space=pl.ANY)
    semaphores = pltpu.SemaphoreType.DMA((count,))
    return pl.pallas_call(
        functools.partial(late_kernel, steps),
        out_shape=pltpu.HBM((features, columns), jnp.bfloat16),
        in_specs=[anywhere, anywhere, pl.BlockSpec(memory_space=pltpu.VMEM)],
        out_specs=anywhere,
        scratch_shapes=[
            pltpu.VMEM((count, features + rows, width), jnp.bfloat16),
            pltpu.VMEM((count, features, width), jnp.bfloat16),
            pltpu.VMEM((features + rows, rows), jnp.float32),
            semaphores, semaphores, semaphores,
        ],
        compiler_params=pltpu.CompilerParams(vmem_limit_bytes=VMEM_LIMIT),
        cost_estimate=pl.CostEstimate(
            flops=2 * rows * columns * (rows + 2 * features),
            bytes_accessed=2 * columns * (rows + 2 * features), transcendentals=0),
        name="late_window",
    )(hidden, base, targets)


OUTER_PARTS = 4


def outer_kernel(place, received, momentum, weights, shard, momentum_out, copies, rs, ms, ws, os_,
                 in_sem, state_sem, copy_sem, out_sem):
    groups, features, width = received.shape
    part_rows = features // OUTER_PARTS
    begin = pl.multiple_of(place[0] * width, 128)
    state = [
        pltpu.make_async_copy(momentum, ms, state_sem.at[0]),
        pltpu.make_async_copy(weights.at[:, pl.ds(begin, width)], ws, state_sem.at[1]),
    ]
    loads = [
        pltpu.make_async_copy(
            received.at[:, pl.ds(part * part_rows, part_rows)],
            rs.at[:, pl.ds(part * part_rows, part_rows)], in_sem.at[part])
        for part in range(OUTER_PARTS)
    ]
    for load in state + loads:
        load.start()
    for load in state:
        load.wait()
    stores = []
    for part in range(OUTER_PARTS):
        rows = pl.ds(part * part_rows, part_rows)
        loads[part].wait()
        total = rs[0, rows].astype(jnp.float32)
        for group in range(1, groups):
            total += rs[group, rows].astype(jnp.float32)
        average = total / groups
        fresh = momentum_rate * ms[rows] + average
        ms[rows] = fresh
        os_[rows] = (
            ws[rows].astype(jnp.float32) - outer_rate * (average + momentum_rate * fresh)
        ).astype(jnp.bfloat16)
        stores += [
            pltpu.make_async_copy(os_.at[rows], copies.at[group, rows], copy_sem.at[part, group])
            for group in range(groups)
        ]
        stores += [
            pltpu.make_async_copy(os_.at[rows], shard.at[rows], out_sem.at[0, part]),
            pltpu.make_async_copy(ms.at[rows], momentum_out.at[rows], out_sem.at[1, part]),
        ]
        for store in stores[-groups - 2:]:
            store.start()
    for store in stores:
        store.wait()


def outer_step(place, received, momentum, weights):
    groups, features, width = received.shape
    anywhere = pl.BlockSpec(memory_space=pl.ANY)
    return pl.pallas_call(
        outer_kernel,
        out_shape=(
            pltpu.HBM(momentum.shape, jnp.bfloat16),
            pltpu.HBM(momentum.shape, jnp.float32),
            pltpu.HBM(received.shape, jnp.bfloat16),
        ),
        in_specs=[pl.BlockSpec(memory_space=pltpu.SMEM)] + [anywhere] * 3,
        out_specs=(anywhere,) * 3,
        scratch_shapes=[
            pltpu.VMEM(received.shape, jnp.bfloat16),
            pltpu.VMEM((features, width), jnp.float32),
            pltpu.VMEM((features, width), jnp.bfloat16),
            pltpu.VMEM((features, width), jnp.bfloat16),
            pltpu.SemaphoreType.DMA((OUTER_PARTS,)),
            pltpu.SemaphoreType.DMA((2,)),
            pltpu.SemaphoreType.DMA((OUTER_PARTS, groups)),
            pltpu.SemaphoreType.DMA((2, OUTER_PARTS)),
        ],
        compiler_params=pltpu.CompilerParams(vmem_limit_bytes=VMEM_LIMIT),
        cost_estimate=pl.CostEstimate(
            flops=groups * features * width, bytes_accessed=4 * groups * features * width,
            transcendentals=0),
        name="outer_step",
    )(place, received, momentum, weights)


def mix_kernel(late, outer, out, late_part, outer_part, mixed, late_sem, outer_sem, out_sem):
    count, _, width = outer.shape

    def columns(piece):
        return pl.ds(piece * width, width)

    loads, stores = [], []
    for piece in range(count):
        loads.append((
            pltpu.make_async_copy(
                late.at[:, columns(piece)], late_part.at[piece], late_sem.at[piece]),
            pltpu.make_async_copy(outer.at[piece], outer_part.at[piece], outer_sem.at[piece])))
        stores.append(pltpu.make_async_copy(
            mixed.at[piece], out.at[:, columns(piece)], out_sem.at[piece]))
        for load in loads[-1]:
            load.start()
    for piece in range(count):
        for load in loads[piece]:
            load.wait()
        mixed[piece] = (
            mixing * late_part[piece].astype(jnp.float32)
            + (1.0 - mixing) * outer_part[piece].astype(jnp.float32)
        ).astype(jnp.bfloat16)
        stores[piece].start()
    for store in stores:
        store.wait()


def mix(late, outer):
    features, columns = late.shape
    anywhere = pl.BlockSpec(memory_space=pl.ANY)
    held = pltpu.VMEM(outer.shape, jnp.bfloat16)
    semaphores = pltpu.SemaphoreType.DMA((PIECES,))
    return pl.pallas_call(
        mix_kernel,
        out_shape=pltpu.HBM((features, columns), jnp.bfloat16),
        in_specs=[anywhere] * 2,
        out_specs=anywhere,
        scratch_shapes=[held] * 3 + [semaphores] * 3,
        compiler_params=pltpu.CompilerParams(vmem_limit_bytes=VMEM_LIMIT),
        cost_estimate=pl.CostEstimate(
            flops=3 * features * columns, bytes_accessed=6 * features * columns,
            transcendentals=0),
        name="mix",
    )(late, outer)


def in_hbm(x):
    return pltpu.with_memory_space_constraint(x, pltpu.HBM)


def body(weights, momentum, hidden, targets):
    features, columns = weights.shape
    width = columns // PIECES
    lanes = lax.axis_size("y")
    depth = lax.axis_size("z")
    cores = lax.axis_size("core")
    own = hidden.reshape(BEFORE + DURING, PIECES, width)

    def near_rows(part, steps):
        return lax.all_gather(part.reshape(steps * PIECES, width), "y", axis=0, tiled=True)

    def target_columns(part, steps):
        parts = part.reshape(steps, depth, lanes, cores, features)
        return parts.transpose(4, 1, 3, 2, 0).reshape(features, -1)

    early_near = near_rows(own[:BEFORE], BEFORE).reshape(2 * lanes * BEFORE, columns // 2)
    early_hidden = lax.all_gather(early_near, RING, axis=0, tiled=True)
    late_near = near_rows(own[BEFORE:], DURING).reshape(lanes * DURING, columns)
    late_hidden = lax.all_gather(late_near, RING, axis=0, tiled=True)
    early_targets = jnp.repeat(target_columns(targets[0, :BEFORE], BEFORE), 2, axis=1)
    late_targets = target_columns(targets[0, BEFORE:], DURING)

    encoded = early_window(BEFORE, early_hidden, weights, early_targets)

    def swap(x):
        return in_hbm(lax.all_to_all(x, REPLICA, split_axis=0, concat_axis=0, tiled=True))

    place = lax.axis_index(REPLICA).astype(jnp.int32)[None]
    outer_shard, momentum_out, copies = outer_step(place, swap(encoded), momentum, weights)
    outer = swap(copies)

    pieces = weights.reshape(features, PIECES, width).transpose(1, 0, 2).astype(jnp.float32)
    base = (pieces - encoded.astype(jnp.float32)).astype(jnp.bfloat16)
    late = late_window(DURING, late_hidden, in_hbm(base), late_targets)
    new_weights = mix(in_hbm(late), outer)[None]
    return (new_weights, outer_shard, momentum_out)


def solution(mesh):
    fine = Mesh(mesh.devices.reshape(8, 4, 2, 2, 4), MESH_AXES)
    placed = (
        P(FSDP, None),
        P(FSDP, REPLICA),
        P(REPLICA, None, FSDP, None),
        P(REPLICA, None, None, FSDP),
    )
    return jax.shard_map(
        body,
        mesh=fine,
        in_specs=placed,
        out_specs=(P(REPLICA, FSDP, None), P(FSDP, REPLICA), P(FSDP, REPLICA)),
        check_vma=False,
    )
```

```python
import functools
import math

import jax
import jax.numpy as jnp
from jax import lax
from jax.experimental import pallas as pl
from jax.experimental.pallas import tpu as pltpu
from jax.sharding import Mesh
from jax.sharding import PartitionSpec as P

BEFORE = 3
DURING = 4

inner_rate = 0.4
outer_rate = 0.7
momentum_rate = 0.9
mixing = 0.5

MESH_AXES = ("z", "y", "core", "y_lo", "x")
FSDP = ("z", "y", "core")
REPLICA = ("y_lo", "x")
RING = ("z", "core")
PIECES = 8
VMEM_LIMIT = 48 * 1024 * 1024
AHEAD = 3
EARLY_PIECE = 1536
EARLY_COUNT = 8
ACROSS = (((1,), (1,)), ((), ()))


def in_order(count, start, use):
    for piece in range(min(AHEAD, count)):
        start(piece)

    def turn(piece, carry):
        @pl.when(piece + AHEAD < count)
        def _():
            start(piece + AHEAD)

        use(piece)
        return carry

    lax.fori_loop(0, count, turn, 0)


def solve(steps, step_of, scaled, gram, wanted, moved_by, total):
    high = gram.astype(jnp.bfloat16)
    low = (gram - high.astype(jnp.float32)).astype(jnp.bfloat16)
    residual = jnp.zeros_like(scaled)
    for number in range(steps):
        moved = scaled
        if number:
            short = residual.astype(jnp.bfloat16)
            product = jnp.dot(short, high, preferred_element_type=jnp.float32)
            product += jnp.dot(short, low, preferred_element_type=jnp.float32)
            moved = scaled - moved_by * total(product)
        fresh = (moved - wanted).astype(jnp.bfloat16).astype(jnp.float32)
        residual = jnp.where(step_of == number, fresh, residual)
    return residual


def early_kernel(steps, parts, *refs):
    hidden = refs[:parts]
    weights, targets, out, held, outs, both_ref, hidden_sem, weights_sem, out_sem = refs[parts:]
    rows = hidden[0].shape[0]
    half = held.shape[1]
    features, columns = weights.shape
    top = 2 * features
    width = columns // PIECES
    inverse_root = 1.0 / math.sqrt(columns)

    pieces, begin = [], 0
    for part in range(parts):
        size = hidden[part].shape[1]
        cuts = 1 if size <= EARLY_PIECE else size // EARLY_PIECE
        for cut in range(cuts):
            pieces.append((part, cut * (size // cuts), begin, size // cuts))
            begin += size // cuts

    def copies(number):
        part, first, place, size = pieces[number]
        yield pltpu.make_async_copy(
            hidden[part].at[:, pl.ds(first, size)],
            held.at[pl.ds(top, rows), pl.ds(place, size)], hidden_sem.at[number])
        for side in range(2):
            yield pltpu.make_async_copy(
                weights.at[:, pl.ds(side * half + place, size)],
                held.at[pl.ds(side * features, features), pl.ds(place, size)],
                weights_sem.at[side, number])

    def out_copy(piece):
        return pltpu.make_async_copy(outs.at[piece], out.at[piece], out_sem.at[piece])

    def start(number):
        for copy in copies(number):
            copy.start()

    for number in range(min(AHEAD, len(pieces))):
        start(number)
    for number, (_, _, place, size) in enumerate(pieces):
        if number + AHEAD < len(pieces):
            start(number + AHEAD)
        for copy in copies(number):
            copy.wait()
        block = pl.ds(place, size)
        product = lax.dot_general(
            held[pl.ds(top, rows), block], held[:, block], ACROSS,
            preferred_element_type=jnp.float32)
        both_ref[...] = product if number == 0 else both_ref[...] + product

    column = lax.broadcasted_iota(jnp.int32, (features, rows), 1)
    left = column % 2 == 0

    def total(x):
        return x + jnp.where(left, pltpu.roll(x, rows - 1, 1), pltpu.roll(x, 1, 1))

    projected = both_ref[:, :top].T
    scaled = total(jnp.where(left, projected[:features], projected[features:])) * inverse_root
    apart = (lax.broadcasted_iota(jnp.int32, (rows, rows), 0)
             + lax.broadcasted_iota(jnp.int32, (rows, rows), 1)) % 2
    gram = jnp.where(apart == 0, both_ref[:, top:], 0.0)
    residual = solve(steps, (column // 2) % steps, scaled, gram, targets[...].astype(jnp.float32),
                     inner_rate * inverse_root * inverse_root, total)
    factors = jnp.concatenate(
        [jnp.where(left, residual, 0.0), jnp.where(left, 0.0, residual)], axis=0
    ).astype(jnp.bfloat16)

    count = half // width
    for piece in range(count):
        update = (inner_rate * inverse_root) * jnp.dot(
            factors, held[pl.ds(top, rows), pl.ds(piece * width, width)],
            preferred_element_type=jnp.float32)
        encoded = update.astype(jnp.bfloat16)
        outs[piece] = encoded[:features]
        outs[count + piece] = encoded[features:]
        out_copy(piece).start()
        out_copy(count + piece).start()
    for piece in range(PIECES):
        out_copy(piece).wait()


def early_window(steps, hidden, weights, targets):
    rows = hidden[0].shape[0]
    features, columns = weights.shape
    width = columns // PIECES
    anywhere = pl.BlockSpec(memory_space=pl.ANY)
    return pl.pallas_call(
        functools.partial(early_kernel, steps, len(hidden)),
        out_shape=pltpu.HBM((PIECES, features, width), jnp.bfloat16),
        in_specs=[anywhere] * (len(hidden) + 1) + [pl.BlockSpec(memory_space=pltpu.VMEM)],
        out_specs=anywhere,
        scratch_shapes=[
            pltpu.VMEM((2 * features + rows, columns // 2), jnp.bfloat16),
            pltpu.VMEM((PIECES, features, width), jnp.bfloat16),
            pltpu.VMEM((rows, 2 * features + rows), jnp.float32),
            pltpu.SemaphoreType.DMA((EARLY_COUNT,)),
            pltpu.SemaphoreType.DMA((2, EARLY_COUNT)),
            pltpu.SemaphoreType.DMA((PIECES,)),
        ],
        compiler_params=pltpu.CompilerParams(vmem_limit_bytes=VMEM_LIMIT),
        cost_estimate=pl.CostEstimate(
            flops=rows * columns * (rows + 4 * features),
            bytes_accessed=columns * (rows + 4 * features), transcendentals=0),
        name="early_window",
    )(*hidden, weights, targets)


def late_kernel(steps, hidden, base, targets, out, held, outs, both_ref, hidden_sem, base_sem,
                out_sem):
    rows = hidden.shape[0]
    count, features, width = base.shape
    inverse_root = 1.0 / math.sqrt(hidden.shape[1])

    def copies(piece):
        yield pltpu.make_async_copy(
            hidden.at[:, pl.ds(piece * width, width)], held.at[piece, pl.ds(features, rows)],
            hidden_sem.at[piece])
        yield pltpu.make_async_copy(
            base.at[piece], held.at[piece, pl.ds(0, features)], base_sem.at[piece])

    def out_copy(piece):
        return pltpu.make_async_copy(
            outs.at[piece], out.at[:, pl.ds(piece * width, width)], out_sem.at[piece])

    def start(piece):
        for copy in copies(piece):
            copy.start()

    def products(piece):
        for copy in copies(piece):
            copy.wait()
        both_ref[...] += lax.dot_general(
            held[piece], held[piece, features:], ACROSS, preferred_element_type=jnp.float32)

    both_ref[...] = jnp.zeros_like(both_ref)
    in_order(count, start, products)

    step_of = lax.broadcasted_iota(jnp.int32, (features, rows), 1) % steps
    residual = solve(steps, step_of, both_ref[:features] * inverse_root, both_ref[features:],
                     targets[...].astype(jnp.float32), inner_rate * inverse_root * inverse_root,
                     lambda x: x)
    factors = residual.astype(jnp.bfloat16)

    def write(piece, carry):
        update = (inner_rate * inverse_root) * jnp.dot(
            factors, held[piece, features:], preferred_element_type=jnp.float32)
        outs[piece] = (held[piece, :features].astype(jnp.float32) - update).astype(jnp.bfloat16)
        out_copy(piece).start()
        return carry

    lax.fori_loop(0, count, write, 0, unroll=4)
    for piece in range(count):
        out_copy(piece).wait()


def late_window(steps, hidden, base, targets):
    rows, columns = hidden.shape
    count, features, width = base.shape
    anywhere = pl.BlockSpec(memory_space=pl.ANY)
    semaphores = pltpu.SemaphoreType.DMA((count,))
    return pl.pallas_call(
        functools.partial(late_kernel, steps),
        out_shape=pltpu.HBM((features, columns), jnp.bfloat16),
        in_specs=[anywhere, anywhere, pl.BlockSpec(memory_space=pltpu.VMEM)],
        out_specs=anywhere,
        scratch_shapes=[
            pltpu.VMEM((count, features + rows, width), jnp.bfloat16),
            pltpu.VMEM((count, features, width), jnp.bfloat16),
            pltpu.VMEM((features + rows, rows), jnp.float32),
            semaphores, semaphores, semaphores,
        ],
        compiler_params=pltpu.CompilerParams(vmem_limit_bytes=VMEM_LIMIT),
        cost_estimate=pl.CostEstimate(
            flops=2 * rows * columns * (rows + 2 * features),
            bytes_accessed=2 * columns * (rows + 2 * features), transcendentals=0),
        name="late_window",
    )(hidden, base, targets)


OUTER_PARTS = 4


def outer_kernel(received, momentum, rows_before, shard, momentum_out, copies, ms, os_, copy_sem,
                 out_sem):
    groups, features, width = received.shape
    part_rows = features // OUTER_PARTS
    stores = []
    for part in range(OUTER_PARTS):
        rows = pl.ds(part * part_rows, part_rows)
        total = received[0, rows].astype(jnp.float32)
        for group in range(1, groups):
            total += received[group, rows].astype(jnp.float32)
        average = total / groups
        fresh = momentum_rate * momentum[rows] + average
        ms[rows] = fresh
        os_[rows] = (
            rows_before[rows].astype(jnp.float32)
            - outer_rate * (average + momentum_rate * fresh)
        ).astype(jnp.bfloat16)
        stores += [
            pltpu.make_async_copy(os_.at[rows], copies.at[group, rows], copy_sem.at[part, group])
            for group in range(groups)
        ]
        stores += [
            pltpu.make_async_copy(os_.at[rows], shard.at[rows], out_sem.at[0, part]),
            pltpu.make_async_copy(ms.at[rows], momentum_out.at[rows], out_sem.at[1, part]),
        ]
        for store in stores[-groups - 2:]:
            store.start()
    for store in stores:
        store.wait()


def outer_step(received, momentum, rows_before):
    groups, features, width = received.shape
    anywhere = pl.BlockSpec(memory_space=pl.ANY)
    return pl.pallas_call(
        outer_kernel,
        out_shape=(
            pltpu.HBM(momentum.shape, jnp.bfloat16),
            pltpu.HBM(momentum.shape, jnp.float32),
            pltpu.HBM(received.shape, jnp.bfloat16),
        ),
        in_specs=[pl.BlockSpec(memory_space=pltpu.VMEM)] * 3,
        out_specs=(anywhere,) * 3,
        scratch_shapes=[
            pltpu.VMEM((features, width), jnp.float32),
            pltpu.VMEM((features, width), jnp.bfloat16),
            pltpu.SemaphoreType.DMA((OUTER_PARTS, groups)),
            pltpu.SemaphoreType.DMA((2, OUTER_PARTS)),
        ],
        compiler_params=pltpu.CompilerParams(vmem_limit_bytes=VMEM_LIMIT),
        cost_estimate=pl.CostEstimate(
            flops=groups * features * width, bytes_accessed=4 * groups * features * width,
            transcendentals=0),
        name="outer_step",
    )(received, momentum, rows_before)


def mix_kernel(late, outer, out, late_part, mixed, late_sem, out_sem):
    count, _, width = outer.shape

    def columns(piece):
        return pl.ds(piece * width, width)

    loads, stores = [], []
    for piece in range(count):
        loads.append(pltpu.make_async_copy(
            late.at[:, columns(piece)], late_part.at[piece], late_sem.at[piece]))
        stores.append(pltpu.make_async_copy(
            mixed.at[piece], out.at[:, columns(piece)], out_sem.at[piece]))
        loads[-1].start()
    for piece in range(count):
        loads[piece].wait()
        mixed[piece] = (
            mixing * late_part[piece].astype(jnp.float32)
            + (1.0 - mixing) * outer[piece].astype(jnp.float32)
        ).astype(jnp.bfloat16)
        stores[piece].start()
    for store in stores:
        store.wait()


def mix(late, outer):
    features, columns = late.shape
    anywhere = pl.BlockSpec(memory_space=pl.ANY)
    held = pltpu.VMEM(outer.shape, jnp.bfloat16)
    semaphores = pltpu.SemaphoreType.DMA((PIECES,))
    return pl.pallas_call(
        mix_kernel,
        out_shape=pltpu.HBM((features, columns), jnp.bfloat16),
        in_specs=[anywhere, pl.BlockSpec(memory_space=pltpu.VMEM)],
        out_specs=anywhere,
        scratch_shapes=[held] * 2 + [semaphores] * 2,
        compiler_params=pltpu.CompilerParams(vmem_limit_bytes=VMEM_LIMIT),
        cost_estimate=pl.CostEstimate(
            flops=3 * features * columns, bytes_accessed=6 * features * columns,
            transcendentals=0),
        name="mix",
    )(late, outer)


def in_hbm(x):
    return pltpu.with_memory_space_constraint(x, pltpu.HBM)


def body(weights, momentum, hidden, targets):
    features, columns = weights.shape
    width = columns // PIECES
    lanes = lax.axis_size("y")
    depth = lax.axis_size("z")
    cores = lax.axis_size("core")
    own = hidden.reshape(BEFORE + DURING, PIECES, width)

    def near_rows(part, steps):
        return lax.all_gather(part.reshape(steps * PIECES, width), "y", axis=0, tiled=True)

    def target_columns(part, steps):
        parts = part.reshape(steps, depth, lanes, cores, features)
        return parts.transpose(4, 1, 3, 2, 0).reshape(features, -1)

    early_near = near_rows(own[:BEFORE], BEFORE).reshape(2 * lanes * BEFORE, columns // 2)
    early_hidden = lax.all_gather(early_near, RING, axis=0, tiled=True)
    late_near = near_rows(own[BEFORE:], DURING).reshape(lanes * DURING, columns)
    late_hidden = lax.all_gather(late_near, RING, axis=0, tiled=True)
    early_targets = jnp.repeat(target_columns(targets[0, :BEFORE], BEFORE), 2, axis=1)
    late_targets = target_columns(targets[0, BEFORE:], DURING)

    encoded = early_window(BEFORE, [early_hidden], weights, early_targets)

    def swap(x):
        return lax.all_to_all(x, REPLICA, split_axis=0, concat_axis=0, tiled=True)

    rows_before = lax.dynamic_slice_in_dim(
        weights, lax.axis_index(REPLICA) * width, width, 1)
    outer_shard, momentum_out, copies = outer_step(swap(encoded), momentum, rows_before)
    outer = swap(copies)

    pieces = weights.reshape(features, PIECES, width).transpose(1, 0, 2).astype(jnp.float32)
    base = (pieces - encoded.astype(jnp.float32)).astype(jnp.bfloat16)
    late = late_window(DURING, late_hidden, in_hbm(base), late_targets)
    new_weights = mix(in_hbm(late), outer)[None]
    return (new_weights, outer_shard, momentum_out)


def solution(mesh):
    fine = Mesh(mesh.devices.reshape(8, 4, 2, 2, 4), MESH_AXES)
    placed = (
        P(FSDP, None),
        P(FSDP, REPLICA),
        P(REPLICA, None, FSDP, None),
        P(REPLICA, None, None, FSDP),
    )
    return jax.shard_map(
        body,
        mesh=fine,
        in_specs=placed,
        out_specs=(P(REPLICA, FSDP, None), P(FSDP, REPLICA), P(FSDP, REPLICA)),
        check_vma=False,
    )
```

```python
import functools
import math

import jax
import jax.numpy as jnp
from jax import lax
from jax.experimental import pallas as pl
from jax.experimental.pallas import tpu as pltpu
from jax.sharding import Mesh
from jax.sharding import PartitionSpec as P

BEFORE = 3
DURING = 4

inner_rate = 0.4
outer_rate = 0.7
momentum_rate = 0.9
mixing = 0.5

MESH_AXES = ("z", "y", "core", "y_lo", "x")
FSDP = ("z", "y", "core")
REPLICA = ("y_lo", "x")
RING = ("z", "core")
PIECES = 8
VMEM_LIMIT=24*1024*1024
SMALL_LIMIT=12*1024*1024
AHEAD = 3
NEAR_PIECES = 4
EARLY_PIECE = 1536
EARLY_COUNT = 8
ACROSS = (((1,), (1,)), ((), ()))


def in_order(count, start, use):
    for piece in range(min(AHEAD, count)):
        start(piece)

    def turn(piece, carry):
        @pl.when(piece + AHEAD < count)
        def _():
            start(piece + AHEAD)

        use(piece)
        return carry

    lax.fori_loop(0, count, turn, 0)


def solve(steps, step_of, scaled, gram, wanted, moved_by, total):
    high = gram.astype(jnp.bfloat16)
    low = (gram - high.astype(jnp.float32)).astype(jnp.bfloat16)
    residual = jnp.zeros_like(scaled)
    for number in range(steps):
        moved = scaled
        if number:
            short = residual.astype(jnp.bfloat16)
            product = jnp.dot(short, high, preferred_element_type=jnp.float32)
            product += jnp.dot(short, low, preferred_element_type=jnp.float32)
            moved = scaled - moved_by * total(product)
        fresh = (moved - wanted).astype(jnp.bfloat16).astype(jnp.float32)
        residual = jnp.where(step_of == number, fresh, residual)
    return residual


def early_kernel(steps, parts, *refs):
    hidden = refs[:parts]
    weights, targets, out, held, outs, both_ref, hidden_sem, weights_sem, out_sem = refs[parts:]
    rows = hidden[0].shape[0]
    half = held.shape[1]
    features, columns = weights.shape
    top = 2 * features
    width = columns // PIECES
    inverse_root = 1.0 / math.sqrt(columns)

    pieces, begin = [], 0
    for part in range(parts):
        size = hidden[part].shape[1]
        cuts = 1 if size <= EARLY_PIECE else size // EARLY_PIECE
        for cut in range(cuts):
            pieces.append((part, cut * (size // cuts), begin, size // cuts))
            begin += size // cuts

    def copies(number):
        part, first, place, size = pieces[number]
        yield pltpu.make_async_copy(
            hidden[part].at[:, pl.ds(first, size)],
            held.at[pl.ds(top, rows), pl.ds(place, size)], hidden_sem.at[number])
        for side in range(2):
            yield pltpu.make_async_copy(
                weights.at[:, pl.ds(side * half + place, size)],
                held.at[pl.ds(side * features, features), pl.ds(place, size)],
                weights_sem.at[side, number])

    def out_copy(piece):
        return pltpu.make_async_copy(outs.at[piece], out.at[piece], out_sem.at[piece])

    def start(number):
        for copy in copies(number):
            copy.start()

    for number in range(min(AHEAD, len(pieces))):
        start(number)
    for number, (_, _, place, size) in enumerate(pieces):
        if number + AHEAD < len(pieces):
            start(number + AHEAD)
        for copy in copies(number):
            copy.wait()
        block = pl.ds(place, size)
        product = lax.dot_general(
            held[pl.ds(top, rows), block], held[:, block], ACROSS,
            preferred_element_type=jnp.float32)
        both_ref[...] = product if number == 0 else both_ref[...] + product

    column = lax.broadcasted_iota(jnp.int32, (features, rows), 1)
    left = column % 2 == 0

    def total(x):
        return x + jnp.where(left, pltpu.roll(x, rows - 1, 1), pltpu.roll(x, 1, 1))

    projected = both_ref[:, :top].T
    scaled = total(jnp.where(left, projected[:features], projected[features:])) * inverse_root
    apart = (lax.broadcasted_iota(jnp.int32, (rows, rows), 0)
             + lax.broadcasted_iota(jnp.int32, (rows, rows), 1)) % 2
    gram = jnp.where(apart == 0, both_ref[:, top:], 0.0)
    residual = solve(steps, (column // 2) % steps, scaled, gram, targets[...].astype(jnp.float32),
                     inner_rate * inverse_root * inverse_root, total)
    factors = jnp.concatenate(
        [jnp.where(left, residual, 0.0), jnp.where(left, 0.0, residual)], axis=0
    ).astype(jnp.bfloat16)

    count = half // width
    for piece in range(count):
        update = (inner_rate * inverse_root) * jnp.dot(
            factors, held[pl.ds(top, rows), pl.ds(piece * width, width)],
            preferred_element_type=jnp.float32)
        encoded = update.astype(jnp.bfloat16)
        outs[piece] = encoded[:features]
        outs[count + piece] = encoded[features:]
        out_copy(piece).start()
        out_copy(count + piece).start()
    for piece in range(PIECES):
        out_copy(piece).wait()


def early_window(steps, hidden, weights, targets):
    rows = hidden[0].shape[0]
    features, columns = weights.shape
    width = columns // PIECES
    anywhere = pl.BlockSpec(memory_space=pl.ANY)
    return pl.pallas_call(
        functools.partial(early_kernel, steps, len(hidden)),
        out_shape=pltpu.HBM((PIECES, features, width), jnp.bfloat16),
        in_specs=[anywhere] * (len(hidden) + 1) + [pl.BlockSpec(memory_space=pltpu.VMEM)],
        out_specs=anywhere,
        scratch_shapes=[
            pltpu.VMEM((2 * features + rows, columns // 2), jnp.bfloat16),
            pltpu.VMEM((PIECES, features, width), jnp.bfloat16),
            pltpu.VMEM((rows, 2 * features + rows), jnp.float32),
            pltpu.SemaphoreType.DMA((EARLY_COUNT,)),
            pltpu.SemaphoreType.DMA((2, EARLY_COUNT)),
            pltpu.SemaphoreType.DMA((PIECES,)),
        ],
        compiler_params=pltpu.CompilerParams(vmem_limit_bytes=VMEM_LIMIT),
        cost_estimate=pl.CostEstimate(
            flops=rows * columns * (rows + 4 * features),
            bytes_accessed=columns * (rows + 4 * features), transcendentals=0),
        name="early_window",
    )(*hidden, weights, targets)


def late_kernel(steps, hidden, base, targets, near, far, held, outs, both_ref, hidden_sem,
                base_sem, out_sem):
    rows = hidden.shape[0]
    count, features, width = base.shape
    inverse_root = 1.0 / math.sqrt(hidden.shape[1])

    def copies(piece):
        yield pltpu.make_async_copy(
            hidden.at[:, pl.ds(piece * width, width)], held.at[piece, pl.ds(features, rows)],
            hidden_sem.at[piece])
        yield pltpu.make_async_copy(
            base.at[piece], held.at[piece, pl.ds(0, features)], base_sem.at[piece])

    def out_copy(piece):
        return pltpu.make_async_copy(outs.at[piece], far.at[piece], out_sem.at[piece])

    def start(piece):
        for copy in copies(piece):
            copy.start()

    def products(piece):
        for copy in copies(piece):
            copy.wait()
        both_ref[...] += lax.dot_general(
            held[piece], held[piece, features:], ACROSS, preferred_element_type=jnp.float32)

    both_ref[...] = jnp.zeros_like(both_ref)
    in_order(count, start, products)

    step_of = lax.broadcasted_iota(jnp.int32, (features, rows), 1) % steps
    residual = solve(steps, step_of, both_ref[:features] * inverse_root, both_ref[features:],
                     targets[...].astype(jnp.float32), inner_rate * inverse_root * inverse_root,
                     lambda x: x)
    factors = residual.astype(jnp.bfloat16)

    kept = near.shape[0]
    for piece in [*range(kept, count), *range(kept)]:
        update = (inner_rate * inverse_root) * jnp.dot(
            factors, held[piece, features:], preferred_element_type=jnp.float32)
        result = (held[piece, :features].astype(jnp.float32) - update).astype(jnp.bfloat16)
        if piece < kept:
            near[piece] = result
        else:
            outs[piece - kept] = result
            out_copy(piece - kept).start()
    for piece in range(count - kept):
        out_copy(piece).wait()


def late_window(steps, hidden, base, targets):
    rows, columns = hidden.shape
    count, features, width = base.shape
    anywhere = pl.BlockSpec(memory_space=pl.ANY)
    semaphores = pltpu.SemaphoreType.DMA((count,))
    far = (count - NEAR_PIECES, features, width)
    return pl.pallas_call(
        functools.partial(late_kernel, steps),
        out_shape=(
            jax.ShapeDtypeStruct((NEAR_PIECES, features, width), jnp.bfloat16),
            pltpu.HBM(far, jnp.bfloat16),
        ),
        in_specs=[anywhere, anywhere, pl.BlockSpec(memory_space=pltpu.VMEM)],
        out_specs=(pl.BlockSpec(memory_space=pltpu.VMEM), anywhere),
        scratch_shapes=[
            pltpu.VMEM((count, features + rows, width), jnp.bfloat16),
            pltpu.VMEM(far, jnp.bfloat16),
            pltpu.VMEM((features + rows, rows), jnp.float32),
            semaphores, semaphores, semaphores,
        ],
        compiler_params=pltpu.CompilerParams(vmem_limit_bytes=VMEM_LIMIT),
        cost_estimate=pl.CostEstimate(
            flops=2 * rows * columns * (rows + 2 * features),
            bytes_accessed=2 * columns * (rows + 2 * features), transcendentals=0),
        name="late_window",
    )(hidden, base, targets)


OUTER_PARTS = 4


def outer_kernel(received, momentum, rows_before, shard, momentum_out, copies, ms, os_, copy_sem,
                 out_sem):
    groups, features, width = received.shape
    part_rows = features // OUTER_PARTS
    stores = []
    for part in range(OUTER_PARTS):
        rows = pl.ds(part * part_rows, part_rows)
        total = received[0, rows].astype(jnp.float32)
        for group in range(1, groups):
            total += received[group, rows].astype(jnp.float32)
        average = total / groups
        fresh = momentum_rate * momentum[rows] + average
        ms[rows] = fresh
        os_[rows] = (
            rows_before[rows].astype(jnp.float32)
            - outer_rate * (average + momentum_rate * fresh)
        ).astype(jnp.bfloat16)
        stores += [
            pltpu.make_async_copy(os_.at[rows], copies.at[group, rows], copy_sem.at[part, group])
            for group in range(groups)
        ]
        stores += [
            pltpu.make_async_copy(os_.at[rows], shard.at[rows], out_sem.at[0, part]),
            pltpu.make_async_copy(ms.at[rows], momentum_out.at[rows], out_sem.at[1, part]),
        ]
        for store in stores[-groups - 2:]:
            store.start()
    for store in stores:
        store.wait()


def outer_step(received, momentum, rows_before):
    groups, features, width = received.shape
    anywhere = pl.BlockSpec(memory_space=pl.ANY)
    return pl.pallas_call(
        outer_kernel,
        out_shape=(
            pltpu.HBM(momentum.shape, jnp.bfloat16),
            pltpu.HBM(momentum.shape, jnp.float32),
            pltpu.HBM(received.shape, jnp.bfloat16),
        ),
        in_specs=[pl.BlockSpec(memory_space=pltpu.VMEM)] * 3,
        out_specs=(anywhere,) * 3,
        scratch_shapes=[
            pltpu.VMEM((features, width), jnp.float32),
            pltpu.VMEM((features, width), jnp.bfloat16),
            pltpu.SemaphoreType.DMA((OUTER_PARTS, groups)),
            pltpu.SemaphoreType.DMA((2, OUTER_PARTS)),
        ],
        compiler_params=pltpu.CompilerParams(vmem_limit_bytes=SMALL_LIMIT),
        cost_estimate=pl.CostEstimate(
            flops=groups * features * width, bytes_accessed=4 * groups * features * width,
            transcendentals=0),
        name="outer_step",
    )(received, momentum, rows_before)


def mix_kernel(near, far, outer, out, late_part, mixed, late_sem, out_sem):
    count, _, width = outer.shape
    kept = near.shape[0]
    loads = [
        pltpu.make_async_copy(far.at[piece], late_part.at[piece], late_sem.at[piece])
        for piece in range(count - kept)
    ]
    for load in loads:
        load.start()
    stores = []
    for piece in range(count):
        if piece < kept:
            late = near[piece]
        else:
            loads[piece - kept].wait()
            late = late_part[piece - kept]
        mixed[piece] = (
            mixing * late.astype(jnp.float32) + (1.0 - mixing) * outer[piece].astype(jnp.float32)
        ).astype(jnp.bfloat16)
        stores.append(pltpu.make_async_copy(
            mixed.at[piece], out.at[:, pl.ds(piece * width, width)], out_sem.at[piece]))
        stores[-1].start()
    for store in stores:
        store.wait()


def mix(near, far, outer):
    count, features, width = outer.shape
    whole = pl.BlockSpec(memory_space=pltpu.VMEM)
    anywhere = pl.BlockSpec(memory_space=pl.ANY)
    return pl.pallas_call(
        mix_kernel,
        out_shape=pltpu.HBM((features, count * width), jnp.bfloat16),
        in_specs=[whole, anywhere, whole],
        out_specs=anywhere,
        scratch_shapes=[
            pltpu.VMEM(far.shape, jnp.bfloat16),
            pltpu.VMEM(outer.shape, jnp.bfloat16),
            pltpu.SemaphoreType.DMA((far.shape[0],)),
            pltpu.SemaphoreType.DMA((count,)),
        ],
        compiler_params=pltpu.CompilerParams(vmem_limit_bytes=SMALL_LIMIT),
        cost_estimate=pl.CostEstimate(
            flops=3 * outer.size, bytes_accessed=6 * outer.size, transcendentals=0),
        name="mix",
    )(near, far, outer)


def in_hbm(x):
    return pltpu.with_memory_space_constraint(x, pltpu.HBM)


def body(weights, momentum, hidden, targets):
    features, columns = weights.shape
    width = columns // PIECES
    lanes = lax.axis_size("y")
    depth = lax.axis_size("z")
    cores = lax.axis_size("core")
    own = lax.optimization_barrier(hidden.reshape(BEFORE + DURING, PIECES, width))

    def near_rows(part, steps):
        return lax.all_gather(part.reshape(steps * PIECES, width), "y", axis=0, tiled=True)

    def target_columns(part, steps):
        parts = part.reshape(steps, depth, lanes, cores, features)
        return parts.transpose(4, 1, 3, 2, 0).reshape(features, -1)

    early_near = near_rows(own[:BEFORE], BEFORE).reshape(2 * lanes * BEFORE, columns // 2)
    early_hidden = lax.all_gather(early_near, RING, axis=0, tiled=True)
    late_near = near_rows(own[BEFORE:], DURING).reshape(lanes * DURING, columns)
    late_hidden = lax.all_gather(late_near, RING, axis=0, tiled=True)
    early_targets = jnp.repeat(target_columns(targets[0, :BEFORE], BEFORE), 2, axis=1)
    late_targets = target_columns(targets[0, BEFORE:], DURING)

    encoded = early_window(BEFORE, [in_hbm(early_hidden)], weights, early_targets)

    def swap(x):
        return lax.all_to_all(x, REPLICA, split_axis=0, concat_axis=0, tiled=True)

    rows_before = lax.dynamic_slice_in_dim(
        weights, lax.axis_index(REPLICA) * width, width, 1)
    outer_shard, momentum_out, copies = outer_step(swap(encoded), momentum, rows_before)
    outer = swap(copies)

    pieces = weights.reshape(features, PIECES, width).transpose(1, 0, 2).astype(jnp.float32)
    base = (pieces - encoded.astype(jnp.float32)).astype(jnp.bfloat16)
    near, far = late_window(DURING, in_hbm(late_hidden), in_hbm(base), late_targets)
    new_weights = mix(near, in_hbm(far), outer)[None]
    return (new_weights, outer_shard, momentum_out)


def solution(mesh):
    fine = Mesh(mesh.devices.reshape(8, 4, 2, 2, 4), MESH_AXES)
    placed = (
        P(FSDP, None),
        P(FSDP, REPLICA),
        P(REPLICA, None, FSDP, None),
        P(REPLICA, None, None, FSDP),
    )
    return jax.shard_map(
        body,
        mesh=fine,
        in_specs=placed,
        out_specs=(P(REPLICA, FSDP, None), P(FSDP, REPLICA), P(FSDP, REPLICA)),
        check_vma=False,
    )
```
